128 devices in a mesh: row: 8 (over x, core), col: 16 (over z, y).
Axes of the slice: x: 4, y: 4, z: 4, core: 2. Of those that a mesh axis runs over, the one named last changes fastest.
Arguments:
- diag_inverse: bfloat16 [2048, 2048], P(('row', 'col')), as said below
- row_left: bfloat16 [8, 2048, 256], P('row', 'col'), may hold values from -3 to 3
- row_right: bfloat16 [8, 2048, 256], P('row', 'col'), may hold values from -0.125 to 0.125
- col_left: bfloat16 [64, 2048, 256], P('col', 'row'), may hold values from -3 to 3
- col_right: bfloat16 [64, 2048, 256], P('col', 'row'), may hold values from -0.125 to 0.125
- row_ranks: int32 [8], P('row'), may hold values from 32 to 256, as said below
- col_ranks: int32 [64], P('col'), may hold values from 32 to 256, as said below
- tile_left: bfloat16 [8, 64, 2048, 256], P('row', 'col'), may hold values from -0.125 to 0.125
- tile_right: bfloat16 [8, 64, 2048, 256], P('row', 'col'), may hold values from -6 to 6
- new_ranks: int32 [8, 64], P('row', 'col'), may hold values from 32 to 256, as said below
Outputs:
- updated: bfloat16 [8, 64, 2048, 256], P('row', 'col')
The draws below stay inside these ranges and needn't reach their ends.
Inputs may be any that keep to these rules, and one draw needn't show every extreme that they name: diag_inverse is lower triangular with diagonal entries between 0.5 and 1.5. `row_ranks`: some panel tile has rank 256 and some has rank 256 // 8. `col_ranks`: some panel tile has rank 256 and some has rank 256 // 8. `new_ranks`: some tile keeps rank 256 and some keeps 256 // 8.
All inputs are finite; a program needn't handle non-finite values.
Results may differ from the reference program's by a relative error of at most 0.0067.
Values may be sent and summed in bfloat16 or wider, within the bound.
A program may use at most 128 MiB of HBM per device.

```python
import math
import jax
import jax.numpy as jnp
from jax import lax

NB = 2048
R = 256
MT = 8
NC = 64


def pin_extremes(key, values, lowest, highest):
    count = values.shape[0]
    first = jax.random.randint(key, (), 0, count)
    values = values.at[first].set(highest)
    return values.at[(first + 1) % count].set(lowest)


def rank_list(key, count):
    first, second = jax.random.split(key)
    values = jax.random.randint(first, (count,), R // 8, R + 1).astype(jnp.int32)
    return pin_extremes(second, values, R // 8, R).astype(jnp.int32)


def draw_row_ranks(key, part):
    key = jax.random.fold_in(key, 11)
    return rank_list(key, MT)


def draw_col_ranks(key, part):
    key = jax.random.fold_in(key, 13)
    return rank_list(key, NC)


def draw_new_ranks(key, part):
    key = jax.random.fold_in(key, 17)
    return rank_list(key, MT * NC).reshape(MT, NC)


def draw_diag_inverse(key, part):
    key = jax.random.fold_in(key, 5)
    first, second = jax.random.split(key)
    rows = lax.broadcasted_iota(jnp.int32, (NB, NB), 0)
    cols = lax.broadcasted_iota(jnp.int32, (NB, NB), 1)
    below = jnp.clip(jax.random.normal(first, (NB, NB), jnp.float32), -5.0, 5.0)
    middle = jax.random.uniform(second, (NB,), jnp.float32, 0.6, 1.4)
    lower = jnp.where(rows > cols, below / math.sqrt(NB), 0.0)
    whole = jnp.where(rows == cols, jnp.broadcast_to(middle[:, None], (NB, NB)), lower)
    return whole.astype(jnp.bfloat16)


def block_scale(key, dims, cuts, smallest, top_value):
    level = 1.0
    for position, shards_of in cuts:
        heights = jax.random.uniform(jax.random.fold_in(jax.random.fold_in(key, 6), position), (shards_of,), jnp.float32, smallest / len(cuts), top_value / len(cuts))
        level = level * jnp.repeat(jnp.exp(heights), dims[position] // shards_of).reshape((-1,) + (1,) * (len(dims) - 1 - position))
    return level


def normal_values(key, extent, spread, most, cuts=(), kind=jnp.bfloat16):
    result = spread * jax.random.normal(key, extent, jnp.float32)
    if cuts:
        result = result * block_scale(key, extent, cuts, -0.22, 0.18)
    return jnp.clip(result, -most, most).astype(kind)


def setup_inputs(seed: int = 0) -> dict:
    arg_keys = jax.random.split(jax.random.key(seed), 11)
    return {
        "diag_inverse": draw_diag_inverse(jax.random.fold_in(arg_keys[10], 71), 0),
        "row_left": normal_values(arg_keys[1], (MT, NB, R), 0.5, 3.0, ((0, 8), (1, 16))),
        "row_right": normal_values(arg_keys[2], (MT, NB, R), NB ** -0.5, 0.125, ((0, 8), (1, 16))),
        "col_left": normal_values(arg_keys[3], (NC, NB, R), 0.5, 3.0, ((0, 16), (1, 8))),
        "col_right": normal_values(arg_keys[4], (NC, NB, R), NB ** -0.5, 0.125, ((0, 16), (1, 8))),
        "row_ranks": draw_row_ranks(jax.random.fold_in(arg_keys[10], 71), 0),
        "col_ranks": draw_col_ranks(jax.random.fold_in(arg_keys[10], 71), 0),
        "tile_left": normal_values(arg_keys[7], (MT, NC, NB, R), NB ** -0.5, 0.125, ((0, 8), (1, 16))),
        "tile_right": normal_values(arg_keys[8], (MT, NC, NB, R), 1.0, 6.0, ((0, 8), (1, 16))),
        "new_ranks": draw_new_ranks(jax.random.fold_in(arg_keys[10], 71), 0),
    }


def solve_panel(diag_inverse, right, ranks):
    retained = (jnp.arange(right.shape[-1], dtype=jnp.int32)[None, :] < ranks[:, None]).astype(jnp.bfloat16)
    masked = right * retained[:, None, :]
    solved = jnp.einsum("nm,tmr->tnr", diag_inverse.astype(jnp.float32), masked.astype(jnp.float32))
    return solved.astype(jnp.bfloat16)


def reference(diag_inverse, row_left, row_right, col_left, col_right, row_ranks, col_ranks, tile_left, tile_right, new_ranks):
    solved_rows = solve_panel(diag_inverse, row_right, row_ranks)
    solved_cols = solve_panel(diag_inverse, col_right, col_ranks).astype(jnp.float32)
    col_left_wide = col_left.astype(jnp.float32)
    rank_width = row_right.shape[-1]

    def update_row(operands):
        left_row, solved_row, left_tiles, right_tiles, ranks_row = operands
        left_tiles = left_tiles.astype(jnp.float32)
        coupling = jnp.einsum("nr,jns->jrs", solved_row.astype(jnp.float32), solved_cols).astype(jnp.bfloat16)
        retained = (jnp.arange(rank_width, dtype=jnp.int32)[None, :] < ranks_row[:, None]).astype(jnp.float32)
        projected = (jnp.einsum("nr,jns->jrs", left_row.astype(jnp.float32), left_tiles) * retained[:, None, :]).astype(jnp.bfloat16)
        gram_matrix = (jnp.einsum("jnr,jns->jrs", left_tiles, left_tiles) * retained[:, None, :]).astype(jnp.bfloat16)
        combined = jnp.einsum("jab,jac->jbc", coupling.astype(jnp.float32), projected.astype(jnp.float32)).astype(jnp.bfloat16)
        first_term = jnp.einsum("jnr,jrs->jns", right_tiles.astype(jnp.float32), gram_matrix.astype(jnp.float32))
        second_term = jnp.einsum("jnb,jbc->jnc", col_left_wide, combined.astype(jnp.float32))
        return (first_term - second_term).astype(jnp.bfloat16)

    return lax.map(update_row, (row_left, solved_rows, tile_left, tile_right, new_ranks))
```

```python
import functools

import jax
import jax.numpy as jnp
from jax import lax
from jax.experimental import pallas as pl
from jax.experimental.pallas import tpu as pltpu
from jax.sharding import PartitionSpec as P

MESH = pl.DeviceIdType.MESH
F32 = jnp.float32
BF16 = jnp.bfloat16

OWN_AHEAD, OWN_BACK, OWN_SIB, PASS_AHEAD, BACK_SIB, AHEAD_SIB, FAR_SIB = range(7)


def dot(a, b):
    return jnp.dot(a, b, preferred_element_type=F32)


def tdot(a, b):
    return lax.dot_general(a, b, (((0,), (0,)), ((), ())), preferred_element_type=F32)


def kernel(
    row_ranks,
    col_ranks,
    new_ranks,
    diag,
    row_left,
    row_right,
    col_left,
    col_right,
    tile_left,
    tile_right,
    out,
    tl,
    tr,
    cr,
    cl,
    rl,
    xr,
    sv,
    yv,
    dr,
    dc,
    gram,
    proj,
    comb,
    res,
    load_sem,
    out_sem,
    x_send,
    x_recv,
    d_send,
    d_recv,
    a_send,
    a_recv,
    g_send,
    g_recv,
):
    r = lax.axis_index("row")
    c = lax.axis_index("col")
    x, k = r // 2, r % 2
    z, y = c // 4, c % 4
    step = 1 - 2 * k
    ahead_x = (x + step + 4) % 4
    back_x = (x - step + 4) % 4
    far_x = (x + 2) % 4
    sib = (2 * x + 1 - k, c)
    ahead = (2 * ahead_x + k, c)
    back = (2 * back_x + k, c)
    far = (2 * far_x + k, c)
    pending = []

    def send(src, dst, ssem, rsem, device):
        copy = pltpu.make_async_remote_copy(
            src_ref=src, dst_ref=dst, send_sem=ssem, recv_sem=rsem, device_id=device, device_id_type=MESH
        )
        copy.start()
        return copy

    barrier = pltpu.get_barrier_semaphore()
    for device in (ahead, back, far, sib):
        pl.semaphore_signal(barrier, inc=1, device_id=device, device_id_type=MESH)
    for d in range(1, 16):
        pl.semaphore_signal(barrier, inc=1, device_id=(r, (c + d) % 16), device_id_type=MESH)

    def load(src, dst, n):
        copy = pltpu.make_async_copy(src, dst, load_sem.at[n])
        copy.start()
        return copy

    load_d = load(diag, dr.at[x, k], 0)
    load_x = load(row_right.at[0], xr.at[z, y], 1)
    load_l = load(row_left.at[0], rl.at[z, y], 2)
    load_tl = [load(tile_left.at[0, j], tl.at[j], 3 + j) for j in range(4)]
    load_cr = load(col_right, cr.at[r], 7)
    load_cl = load(col_left, cl.at[r], 8)
    load_tr = load(tile_right.at[0], tr, 9)
    pl.semaphore_wait(barrier, 19)

    def gather_first(n, src, buf):
        copies = []
        for d in range(1, 4):
            for h, device in ((0, (r, 4 * z + (y + d) % 4)), (1, (r, 4 * ((z + d) % 4) + y))):
                rows = pl.ds(64 * h, 64)
                s = 6 * h + d - 1
                copies.append(
                    send(src.at[rows], buf.at[z, y, rows], g_send.at[n, s], g_recv.at[n, s], device)
                )
        pending.extend(copies)
        return copies

    def gather_second(n, buf, firsts):
        for copy in firsts:
            copy.wait_recv()
        copies = []
        for d in range(1, 4):
            part = buf.at[z, :, pl.ds(0, 64)]
            copies.append(send(part, part, g_send.at[n, 2 + d], g_recv.at[n, 2 + d], (r, 4 * ((z + d) % 4) + y)))
            part = buf.at[:, y, pl.ds(64, 64)]
            copies.append(send(part, part, g_send.at[n, 8 + d], g_recv.at[n, 8 + d], (r, 4 * z + (y + d) % 4)))
        pending.extend(copies)
        return copies

    def wait_all(copies):
        for copy in copies:
            copy.wait_recv()

    panels = (cr, cl)

    def panel_copy(kind, t, j, slot, device):
        ref = panels[t].at[slot, j]
        s = 4 * t + j
        return pltpu.make_async_remote_copy(
            src_ref=ref, dst_ref=ref, send_sem=x_send.at[kind, s], recv_sem=x_recv.at[kind, s],
            device_id=device, device_id_type=MESH,
        )

    def panel_own(t, j):
        panel_copy(OWN_AHEAD, t, j, r, ahead).start()
        panel_copy(OWN_BACK, t, j, r, back).start()
        panel_copy(OWN_SIB, t, j, r, sib).start()

    back_slot = 2 * back_x + k
    ahead_slot = 2 * ahead_x + k
    far_slot = 2 * far_x + k

    def panel_pass(t, j):
        panel_copy(OWN_AHEAD, t, j, back_slot, ahead).wait_recv()
        panel_copy(PASS_AHEAD, t, j, back_slot, ahead).start()
        panel_copy(BACK_SIB, t, j, back_slot, sib).start()
        panel_copy(OWN_BACK, t, j, ahead_slot, back).wait_recv()
        panel_copy(AHEAD_SIB, t, j, ahead_slot, sib).start()

    def panel_far(t, j):
        panel_copy(PASS_AHEAD, t, j, far_slot, ahead).wait_recv()
        panel_copy(FAR_SIB, t, j, far_slot, sib).start()

    d_own = [
        send(diag, dr.at[x, k], d_send.at[n], d_recv.at[n], device) for n, device in enumerate((ahead, back, far))
    ]
    pending.extend(d_own)
    x_first = gather_first(0, row_right.at[0], xr)
    load_cr.wait()
    for j in range(4):
        panel_own(0, j)
    load_cl.wait()
    panel_own(1, 0)
    l_first = gather_first(1, row_left.at[0], rl)

    def local_products(j):
        load_tl[j].wait()
        g = tdot(tl[j], tl[j])
        keep = lax.broadcasted_iota(jnp.int32, (256, 256), 1) < new_ranks[0, j]
        gram[j] = jnp.where(keep, g, 0.0).astype(BF16)

    load_x.wait()
    x_second = gather_second(0, xr, x_first)

    load_d.wait()
    wait_all(d_own)
    share = dr.at[:, k]
    d_share = send(share, share, d_send.at[3], d_recv.at[3], sib)
    pending.append(d_share)
    local_products(0)
    d_share.wait_recv()
    half = pl.ds(2 * k, 2)
    for d in range(1, 16):
        dest = (c + d) % 16
        pending.append(
            send(
                dr.at[half, :, :, pl.ds(pl.multiple_of(dest * 128, 128), 128)],
                dc.at[c, half],
                a_send.at[d],
                a_recv.at[d],
                (r, dest),
            )
        )
    a_copies = pending[-15:]
    d_local = load(dr.at[half, :, :, pl.ds(pl.multiple_of(c * 128, 128), 128)], dc.at[c, half], 0)
    local_products(1)

    wait_all(x_second)
    solved = jnp.zeros((128, 256), F32)
    for m in range(8):
        a = dr[:, :, :, 256 * m : 256 * m + 256].reshape(128, 256)
        solved += dot(a, xr[m // 2, 2 * (m % 2) : 2 * (m % 2) + 2].reshape(256, 256))
    sv[z, y] = solved.astype(BF16)
    s_first = gather_first(2, sv.at[z, y], sv)
    load_l.wait()
    l_second = gather_second(1, rl, l_first)
    for j in range(2):
        panel_pass(0, j)
        panel_own(1, j + 1)
    wait_all(a_copies)
    d_local.wait()
    share = dc.at[:, half]
    c_share = send(share, share, a_send.at[0], a_recv.at[0], sib)
    pending.append(c_share)
    s_second = gather_second(2, sv, s_first)
    local_products(2)
    panel_pass(0, 2)
    panel_own(1, 3)
    panel_pass(0, 3)
    local_products(3)
    c_share.wait_recv()

    wait_all(s_second)
    yslab = jnp.zeros((128, 256), F32)
    for m in range(8):
        a = dc[2 * m : 2 * m + 2].reshape(256, 128)
        yslab += tdot(a, sv[m // 2, 2 * (m % 2) : 2 * (m % 2) + 2].reshape(256, 256))
    yv[z, y] = yslab.astype(BF16)
    y_first = gather_first(3, yv.at[z, y], yv)
    wait_all(l_second)

    def projected(j):
        p = jnp.zeros((256, 256), F32)
        for m in range(8):
            a = rl[m // 2, 2 * (m % 2) : 2 * (m % 2) + 2].reshape(256, 256)
            p += tdot(a, tl[j, 256 * m : 256 * m + 256])
        proj[j] = p.astype(BF16)

    projected(0)
    y_second = gather_second(3, yv, y_first)
    for j in range(1, 4):
        projected(j)
    for j in range(4):
        panel_pass(1, j)
    for j in range(4):
        panel_far(0, j)
    for j in range(4):
        for kind, slot in ((OWN_SIB, r), (BACK_SIB, r), (AHEAD_SIB, r), (FAR_SIB, r)):
            panel_copy(kind, 0, j, slot, sib).wait_recv()

    wait_all(y_second)
    for j in range(4):
        g = jnp.zeros((256, 256), F32)
        for m in range(8):
            a = yv[m // 2, 2 * (m % 2) : 2 * (m % 2) + 2].reshape(256, 256)
            g += tdot(a, cr[m, j])
        keep = (lax.broadcasted_iota(jnp.int32, (256, 256), 0) < row_ranks[0]) & (
            lax.broadcasted_iota(jnp.int32, (256, 256), 1) < col_ranks[j]
        )
        coupling = jnp.where(keep, g, 0.0).astype(BF16)
        cm = tdot(coupling, proj[j])
        keep = lax.broadcasted_iota(jnp.int32, (256, 256), 1) < new_ranks[0, j]
        comb[j] = jnp.where(keep, cm, 0.0).astype(BF16)

    def out_copy(slot, j):
        rows = pl.ds(pl.multiple_of(slot * 256, 256), 256)
        return pltpu.make_async_copy(res.at[j, rows], out.at[0, j, rows], out_sem.at[slot, j])

    def update(slot, j):
        rows = pl.ds(pl.multiple_of(slot * 256, 256), 256)
        res[j, rows, :] = (dot(tr[j, rows, :], gram[j]) - dot(cl[slot, j], comb[j])).astype(BF16)
        out_copy(slot, j).start()

    load_tr.wait()
    sib_slot = 2 * x + 1 - k
    sib_back_slot = 2 * ahead_x + 1 - k
    sib_ahead_slot = 2 * back_x + 1 - k
    sib_far_slot = 2 * far_x + 1 - k
    for slot in (r, back_slot, ahead_slot):
        for j in range(4):
            update(slot, j)
    for kind, slot in ((OWN_SIB, sib_slot), (BACK_SIB, sib_back_slot), (AHEAD_SIB, sib_ahead_slot)):
        for j in range(4):
            panel_copy(kind, 1, j, r, sib).wait_recv()
            update(slot, j)
    for j in range(4):
        panel_far(1, j)
        update(far_slot, j)
        panel_copy(FAR_SIB, 1, j, r, sib).wait_recv()
        update(sib_far_slot, j)

    for copy in pending:
        copy.wait_send()
    for t in range(2):
        for j in range(4):
            for kind in range(7):
                panel_copy(kind, t, j, r, sib).wait_send()
    for slot in range(8):
        for j in range(4):
            out_copy(slot, j).wait()


def on_device(
    diag_inverse, row_left, row_right, col_left, col_right, row_ranks, col_ranks, tile_left, tile_right, new_ranks
):
    hbm = pl.BlockSpec(memory_space=pl.ANY)
    smem = pl.BlockSpec(memory_space=pltpu.SMEM)
    dma = pltpu.SemaphoreType.DMA
    return pl.pallas_call(
        kernel,
        out_shape=jax.ShapeDtypeStruct(tile_right.shape, tile_right.dtype),
        in_specs=[smem] * 3 + [hbm] * 7,
        out_specs=hbm,
        scratch_shapes=[
            pltpu.VMEM((4, 2048, 256), BF16),
            pltpu.VMEM((4, 2048, 256), BF16),
            pltpu.VMEM((8, 4, 256, 256), BF16),
            pltpu.VMEM((8, 4, 256, 256), BF16),
            pltpu.VMEM((4, 4, 128, 256), BF16),
            pltpu.VMEM((4, 4, 128, 256), BF16),
            pltpu.VMEM((4, 4, 128, 256), BF16),
            pltpu.VMEM((4, 4, 128, 256), BF16),
            pltpu.VMEM((4, 2, 16, 2048), BF16),
            pltpu.VMEM((16, 4, 2, 16, 128), BF16),
            pltpu.VMEM((4, 256, 256), BF16),
            pltpu.VMEM((4, 256, 256), BF16),
            pltpu.VMEM((4, 256, 256), BF16),
            pltpu.VMEM((4, 2048, 256), BF16),
            dma((10,)),
            dma((8, 4)),
            dma((7, 8)),
            dma((7, 8)),
            dma((4,)),
            dma((4,)),
            dma((16,)),
            dma((16,)),
            dma((4, 12)),
            dma((4, 12)),
        ],
        compiler_params=pltpu.CompilerParams(
            collective_id=0, has_side_effects=True, vmem_limit_bytes=60 * 1024 * 1024
        ),
        name="panel_step",
    )(
        row_ranks, col_ranks, new_ranks, diag_inverse, row_left, row_right, col_left, col_right, tile_left, tile_right
    )


def solution(mesh):
    in_specs = (
        P(("row", "col"), None),
        P("row", "col", None),
        P("row", "col", None),
        P("col", "row", None),
        P("col", "row", None),
        P("row"),
        P("col"),
        P("row", "col", None, None),
        P("row", "col", None, None),
        P("row", "col"),
    )
    out_specs = P("row", "col", None, None)
    return jax.shard_map(on_device, mesh=mesh, in_specs=in_specs, out_specs=out_specs, check_vma=False)
```

```python
import functools

import jax
import jax.numpy as jnp
from jax import lax
from jax.experimental import pallas as pl
from jax.experimental.pallas import tpu as pltpu
from jax.sharding import PartitionSpec as P

MESH = pl.DeviceIdType.MESH
F32 = jnp.float32
BF16 = jnp.bfloat16

OWN_AHEAD, OWN_BACK, OWN_SIB, PASS_AHEAD, BACK_SIB, AHEAD_SIB, FAR_SIB = range(7)


def dot(a, b):
    return jnp.dot(a, b, preferred_element_type=F32)


def tdot(a, b):
    return lax.dot_general(a, b, (((0,), (0,)), ((), ())), preferred_element_type=F32)


def remote(group, src, dst, ssem, rsem, device):
    return pltpu.make_async_remote_copy(
        src_ref=src, dst_ref=dst, send_sem=ssem, recv_sem=rsem, device_id=device, device_id_type=MESH
    )


def kernel(
    row_ranks,
    col_ranks,
    new_ranks,
    diag,
    row_left,
    row_right,
    col_left,
    col_right,
    tile_left,
    tile_right,
    out,
    tl,
    tr,
    cr,
    cl,
    rl,
    xr,
    yacc,
    yt,
    dm,
    gram,
    coup,
    comb,
    term,
    rank_c,
    rank_n,
    load_sem,
    x_send,
    x_recv,
    d_send,
    d_recv,
    a_send,
    a_recv,
    g_send,
    g_recv,
):
    r = lax.axis_index("row")
    c = lax.axis_index("col")
    x, k = r // 2, r % 2
    z, y = c // 4, c % 4
    step = 1 - 2 * k
    ahead_x = (x + step + 4) % 4
    back_x = (x - step + 4) % 4
    far_x = (x + 2) % 4
    sib = (2 * x + 1 - k, c)
    ahead = (2 * ahead_x + k, c)
    back = (2 * back_x + k, c)
    far = (2 * far_x + k, c)
    pending = []

    def send(group, src, dst, ssem, rsem, device):
        copy = remote(group, src, dst, ssem, rsem, device)
        copy.start()
        return copy

    barrier = pltpu.get_barrier_semaphore()
    for device in (ahead, back, far, sib):
        pl.semaphore_signal(barrier, inc=1, device_id=device, device_id_type=MESH)
    for d in range(1, 4):
        for device in ((r, 4 * z + (y + d) % 4), (r, 4 * ((z + d) % 4) + y)):
            pl.semaphore_signal(barrier, inc=1, device_id=device, device_id_type=MESH)

    def load(src, dst, n):
        copy = pltpu.make_async_copy(src, dst, load_sem.at[n])
        copy.start()
        return copy

    load_ranks = [load(col_ranks, rank_c, 10), load(new_ranks, rank_n, 11)]
    load_x = load(row_right.at[0], xr.at[z, y], 1)
    load_d = load(diag, dm.at[x, k, z, y], 0)
    load_tl = [load(tile_left.at[0, j], tl.at[j], 3 + j) for j in range(4)]
    load_l = load(row_left.at[0], rl.at[z, y], 2)
    load_cr = load(col_right, cr.at[:, r], 7)
    load_cl = load(col_left, cl.at[:, 0, k], 8)
    load_tr = load(tile_right.at[0], tr, 9)
    pl.semaphore_wait(barrier, 10)

    def gather_first(n, sources, view):
        copies = []
        for d in range(1, 4):
            for h, device in ((0, (r, 4 * z + (y + d) % 4)), (1, (r, 4 * ((z + d) % 4) + y))):
                s = 3 * h + d - 1
                copies.append(send("gather", sources[h], view(h, z, y), g_send.at[n, s], g_recv.at[n, s], device))
        pending.extend(copies)
        return copies

    def gather_second(n, view, firsts):
        wait_all(firsts)
        halves = []
        for e, d in ((0, 1), (1, 3)):
            for half in (e, 1 - e):
                pair = pl.ds(2 * half, 2)
                for h, device in ((0, (r, 4 * ((z + d) % 4) + y)), (1, (r, 4 * z + (y + d) % 4))):
                    part = view(0, z, pair) if h == 0 else view(1, pair, y)
                    s = 6 + 4 * h + 2 * e + half
                    copy = send("gather", part, part, g_send.at[n, s], g_recv.at[n, s], device)
                    halves.append((copy, h, e, d, half))
                    pending.append(copy)
        return halves

    def gather_relay(n, view, halves):
        copies = []
        for copy, h, e, d, half in halves:
            if half != e:
                copies.append(copy)
                continue
            copy.wait_recv()
            pair = pl.ds(2 * half, 2)
            if h == 0:
                part, device = view(0, (z - d + 4) % 4, pair), (r, 4 * ((z + d) % 4) + y)
            else:
                part, device = view(1, pair, (y - d + 4) % 4), (r, 4 * z + (y + d) % 4)
            s = 14 + 2 * h + e
            relayed = send("gather", part, part, g_send.at[n, s], g_recv.at[n, s], device)
            copies.append(relayed)
            pending.append(relayed)
        return copies

    def wait_all(copies):
        for copy in copies:
            copy.wait_recv()

    def slab_view(buf):
        return lambda h, zz, yy: buf.at[zz, yy, pl.ds(64 * h, 64)]

    def diag_view(p):
        width = 256 * (p + 1)
        return lambda h, zz, yy: dm.at[p, k, zz, yy, :, pl.ds(width * h, width)]

    back_slot = 2 * back_x + k
    ahead_slot = 2 * ahead_x + k
    far_slot = 2 * far_x + k

    def panel_copy(kind, t, j):
        if t == 0:
            slot = {PASS_AHEAD: back_slot, BACK_SIB: back_slot, AHEAD_SIB: ahead_slot, FAR_SIB: far_slot}.get(kind, r)
            src = dst = cr.at[j, slot]
        else:
            here = {PASS_AHEAD: 2 - k, BACK_SIB: 2 - k, AHEAD_SIB: 1 + k, FAR_SIB: 3}.get(kind, 0)
            there = {OWN_AHEAD: 2 - k, OWN_BACK: 1 + k, PASS_AHEAD: 3}.get(kind, here)
            src, dst = cl.at[j, here, k], cl.at[j, there, k]
        device = {OWN_AHEAD: ahead, PASS_AHEAD: ahead, OWN_BACK: back}.get(kind, sib)
        s = 4 * t + j
        return remote("panel", src, dst, x_send.at[kind, s], x_recv.at[kind, s], device)

    def panel_own(t, j):
        for kind in (OWN_AHEAD, OWN_BACK, OWN_SIB):
            panel_copy(kind, t, j).start()

    def panel_pass(t, j):
        panel_copy(OWN_AHEAD, t, j).wait_recv()
        panel_copy(PASS_AHEAD, t, j).start()
        panel_copy(BACK_SIB, t, j).start()
        panel_copy(OWN_BACK, t, j).wait_recv()
        panel_copy(AHEAD_SIB, t, j).start()

    def panel_far(t, j):
        panel_copy(PASS_AHEAD, t, j).wait_recv()
        panel_copy(FAR_SIB, t, j).start()

    def panel_sibling(t, j, kinds):
        for kind in kinds:
            panel_copy(kind, t, j).wait_recv()

    for p in range(4):

        @pl.when(x == p)
        def _():
            for n, device in enumerate((ahead, back, far)):
                part = pl.ds(0, 512 * (p + 1))
                send("diag", diag.at[:, part], dm.at[p, k, z, y, :, part], d_send.at[n], d_recv.at[p], device)

    x_view, l_view = slab_view(xr), slab_view(rl)
    d_view = [diag_view(p) for p in range(4)]
    x_first = gather_first(0, [row_right.at[0, pl.ds(64 * h, 64)] for h in range(2)], x_view)
    l_first = gather_first(1, [row_left.at[0, pl.ds(64 * h, 64)] for h in range(2)], l_view)
    load_cr.wait()
    load_cl.wait()
    for j in range(4):
        panel_own(0, j)
    for j in range(4):
        panel_own(1, j)

    def local_products(j):
        load_tl[j].wait()
        g = tdot(tl[j], tl[j])
        keep = lax.broadcasted_iota(jnp.int32, (256, 256), 1) < rank_n[0, j]
        gram[j] = jnp.where(keep, g, 0.0).astype(BF16)

    def diag_share(p):
        wait_all(d_relay[p])
        part = dm.at[p, k, :, :, :, pl.ds(0, 512 * (p + 1))]
        copy = send("diag", part, part, a_send.at[p], a_recv.at[p], sib)
        pending.append(copy)
        return copy

    def solve(p):
        width = 512 * (p + 1)
        a = dm[p, :, :, :, :, 0:width].reshape(512, width)
        solved = dot(a, xr[0 : p + 1].reshape(width, 256)).astype(BF16).T
        for b in range(p + 1):
            cols = slice(512 * b, 512 * b + 512)
            acc = dot(solved, dm[p, :, :, :, :, cols].reshape(512, 512))
            if p < 3:
                acc += yacc[:, cols]
            if b == p:
                yt[:, cols] = acc.astype(BF16)
            else:
                yacc[:, cols] = acc

    chips = (x, (x + 1) % 4, (x + 3) % 4, far_x)

    def chip_rows(i):
        return pl.ds(pl.multiple_of(chips[i] * 512, 512), 512)

    def first_term(j):
        for i in range(4):
            term[j, i] = dot(tr[j, chip_rows(i), :], gram[j])

    for copy in load_ranks:
        copy.wait()
    local_products(0)
    load_x.wait()
    x_second = gather_second(0, x_view, x_first)
    load_d.wait()
    d_first, d_second, d_relay = {}, {}, {}
    for p in (3, 2, 1, 0):

        @pl.when(x != p)
        def _():
            part = dm.at[p, k, z, y, :, pl.ds(0, 512 * (p + 1))]
            remote("diag", part, part, d_send.at[0], d_recv.at[p], far).wait_recv()

        d_first[p] = gather_first(2 + p, [d_view[p](h, z, y) for h in range(2)], d_view[p])
    local_products(1)
    panel_pass(0, 0)
    local_products(2)
    x_relay = gather_relay(0, x_view, x_second)
    panel_pass(0, 1)
    local_products(3)
    for p in (3, 2, 1, 0):
        d_second[p] = gather_second(2 + p, d_view[p], d_first[p])
    load_tr.wait()
    first_term(0)
    panel_pass(0, 2)
    first_term(1)
    first_term(2)
    panel_pass(0, 3)
    first_term(3)
    wait_all(x_relay)
    panel_pass(1, 0)
    d_relay[3] = gather_relay(5, d_view[3], d_second[3])
    panel_pass(1, 1)
    for p in (2, 1, 0):
        d_relay[p] = gather_relay(2 + p, d_view[p], d_second[p])
    load_l.wait()
    l_second = gather_second(1, l_view, l_first)
    panel_pass(1, 2)
    shares = {3: diag_share(3)}
    panel_pass(1, 3)
    shares[2] = diag_share(2)
    shares[3].wait_recv()
    solve(3)
    shares.update({p: diag_share(p) for p in (1, 0)})
    shares[2].wait_recv()
    solve(2)
    l_relay = gather_relay(1, l_view, l_second)
    for p in (1, 0):
        shares[p].wait_recv()
        solve(p)
    for j in range(4):
        panel_far(0, j)

    for j in range(4):
        panel_sibling(0, j, (OWN_SIB, BACK_SIB, AHEAD_SIB, FAR_SIB))
        g = dot(yt[...], cr[j].reshape(2048, 256))
        keep = (lax.broadcasted_iota(jnp.int32, (256, 256), 0) < row_ranks[0]) & (
            lax.broadcasted_iota(jnp.int32, (256, 256), 1) < rank_c[j]
        )
        coup[j] = jnp.where(keep, g, 0.0).astype(BF16).T
    wait_all(l_relay)
    for j in range(4):
        projected = tdot(rl[...].reshape(2048, 256), tl[j]).astype(BF16)
        cm = dot(coup[j], projected)
        keep = lax.broadcasted_iota(jnp.int32, (256, 256), 1) < rank_n[0, j]
        comb[j] = jnp.where(keep, cm, 0.0).astype(BF16)

    def update(i, j):
        second = dot(cl[j, i].reshape(512, 256), comb[j])
        out[0, j, chip_rows(i), :] = (term[j, i] - second).astype(BF16)

    for j in range(4):
        panel_far(1, j)
        panel_sibling(1, j, (OWN_SIB, BACK_SIB, AHEAD_SIB))
        for i in range(3):
            update(i, j)
    for j in range(4):
        panel_sibling(1, j, (FAR_SIB,))
        update(3, j)

    for p in range(4):

        @pl.when(x == p)
        def _():
            for n in range(3):
                part = dm.at[p, k, z, y, :, pl.ds(0, 512 * (p + 1))]
                remote("diag", part, part, d_send.at[n], d_recv.at[p], far).wait_send()

    for copy in pending:
        copy.wait_send()
    for t in range(2):
        for j in range(4):
            for kind in range(7):
                panel_copy(kind, t, j).wait_send()


def on_device(
    diag_inverse, row_left, row_right, col_left, col_right, row_ranks, col_ranks, tile_left, tile_right, new_ranks
):
    hbm = pl.BlockSpec(memory_space=pltpu.HBM)
    operands = (
        col_ranks, new_ranks, diag_inverse, row_left, row_right, col_left, col_right, tile_left, tile_right
    )
    dma = pltpu.SemaphoreType.DMA
    return pl.pallas_call(
        kernel,
        out_shape=pltpu.VMEM(tile_right.shape, tile_right.dtype),
        in_specs=[pl.BlockSpec(memory_space=pltpu.SMEM)] + [hbm] * 9,
        out_specs=pl.BlockSpec(memory_space=pltpu.VMEM),
        scratch_shapes=[
            pltpu.VMEM((4, 2048, 256), BF16),
            pltpu.VMEM((4, 2048, 256), BF16),
            pltpu.VMEM((4, 8, 256, 256), BF16),
            pltpu.VMEM((4, 4, 2, 256, 256), BF16),
            pltpu.VMEM((4, 4, 128, 256), BF16),
            pltpu.VMEM((4, 4, 128, 256), BF16),
            pltpu.VMEM((256, 1536), F32),
            pltpu.VMEM((256, 2048), BF16),
            pltpu.VMEM((4, 2, 4, 4, 16, 2048), BF16),
            pltpu.VMEM((4, 256, 256), BF16),
            pltpu.VMEM((4, 256, 256), BF16),
            pltpu.VMEM((4, 256, 256), BF16),
            pltpu.VMEM((4, 4, 512, 256), F32),
            pltpu.SMEM((4,), jnp.int32),
            pltpu.SMEM((1, 4), jnp.int32),
            dma((12,)),
            dma((7, 8)),
            dma((7, 8)),
            dma((3,)),
            dma((4,)),
            dma((4,)),
            dma((4,)),
            dma((6, 18)),
            dma((6, 18)),
        ],
        compiler_params=pltpu.CompilerParams(
            collective_id=0, has_side_effects=True, vmem_limit_bytes=52 * 1024 * 1024
        ),
        name="panel_step",
    )(row_ranks, *[pltpu.with_memory_space_constraint(a, pltpu.HBM) for a in operands])


def solution(mesh):
    in_specs = (
        P(("row", "col"), None),
        P("row", "col", None),
        P("row", "col", None),
        P("col", "row", None),
        P("col", "row", None),
        P("row"),
        P("col"),
        P("row", "col", None, None),
        P("row", "col", None, None),
        P("row", "col"),
    )
    out_specs = P("row", "col", None, None)
    return jax.shard_map(on_device, mesh=mesh, in_specs=in_specs, out_specs=out_specs, check_vma=False)
```

```python
import functools

import jax
import jax.numpy as jnp
from jax import lax
from jax.experimental import pallas as pl
from jax.experimental.pallas import tpu as pltpu
from jax.sharding import PartitionSpec as P

MESH = pl.DeviceIdType.MESH
F32 = jnp.float32
BF16 = jnp.bfloat16

OWN_AHEAD, OWN_BACK, OWN_SIB, PASS_AHEAD, BACK_SIB, AHEAD_SIB, FAR_SIB = range(7)


def dot(a, b):
    return jnp.dot(a, b, preferred_element_type=F32)


def tdot(a, b):
    return lax.dot_general(a, b, (((0,), (0,)), ((), ())), preferred_element_type=F32)


def remote(group, src, dst, ssem, rsem, device):
    return pltpu.make_async_remote_copy(
        src_ref=src, dst_ref=dst, send_sem=ssem, recv_sem=rsem, device_id=device, device_id_type=MESH
    )


def kernel(
    row_ranks,
    col_ranks,
    new_ranks,
    diag,
    row_left,
    row_right,
    col_left,
    col_right,
    tile_left,
    tile_right,
    out,
    tl,
    tr,
    cr,
    cl,
    rl,
    xr,
    st,
    yt,
    dm,
    gram,
    coup,
    comb,
    term,
    rank_c,
    rank_n,
    load_sem,
    x_send,
    x_recv,
    d_send,
    d_recv,
    a_send,
    a_recv,
    g_send,
    g_recv,
):
    r = lax.axis_index("row")
    c = lax.axis_index("col")
    x, k = r // 2, r % 2
    z, y = c // 4, c % 4
    step = 1 - 2 * k
    ahead_x = (x + step + 4) % 4
    back_x = (x - step + 4) % 4
    far_x = (x + 2) % 4
    sib = (2 * x + 1 - k, c)
    ahead = (2 * ahead_x + k, c)
    back = (2 * back_x + k, c)
    far = (2 * far_x + k, c)
    pending = []

    def send(group, src, dst, ssem, rsem, device):
        copy = remote(group, src, dst, ssem, rsem, device)
        copy.start()
        return copy

    barrier = pltpu.get_barrier_semaphore()
    for device in (ahead, back, far, sib):
        pl.semaphore_signal(barrier, inc=1, device_id=device, device_id_type=MESH)
    for d in range(1, 4):
        for device in ((r, 4 * z + (y + d) % 4), (r, 4 * ((z + d) % 4) + y)):
            pl.semaphore_signal(barrier, inc=1, device_id=device, device_id_type=MESH)

    def load(src, dst, n):
        copy = pltpu.make_async_copy(src, dst, load_sem.at[n])
        copy.start()
        return copy

    load_ranks = [load(col_ranks, rank_c, 10), load(new_ranks, rank_n, 11)]
    load_x = load(row_right.at[0], xr.at[z, y], 1)
    load_d = load(diag, dm.at[x, k, z, y], 0)
    load_tl = [load(tile_left.at[0, j], tl.at[j], 3 + j) for j in range(4)]
    load_l = load(row_left.at[0], rl.at[z, y], 2)
    load_cr = load(col_right, cr.at[:, r], 7)
    load_cl = load(col_left, cl.at[:, 0, k], 8)
    load_tr = load(tile_right.at[0], tr, 9)
    pl.semaphore_wait(barrier, 10)

    def gather_first(n, sources, view):
        copies = []
        for d in range(1, 4):
            for h, device in ((0, (r, 4 * z + (y + d) % 4)), (1, (r, 4 * ((z + d) % 4) + y))):
                s = 3 * h + d - 1
                copies.append(send("gather", sources[h], view(h, z, y), g_send.at[n, s], g_recv.at[n, s], device))
        pending.extend(copies)
        return copies

    def gather_second(n, view, firsts):
        wait_all(firsts)
        halves = []
        for e, d in ((0, 1), (1, 3)):
            for half in (e, 1 - e):
                pair = pl.ds(2 * half, 2)
                for h, device in ((0, (r, 4 * ((z + d) % 4) + y)), (1, (r, 4 * z + (y + d) % 4))):
                    part = view(0, z, pair) if h == 0 else view(1, pair, y)
                    s = 6 + 4 * h + 2 * e + half
                    copy = send("gather", part, part, g_send.at[n, s], g_recv.at[n, s], device)
                    halves.append((copy, h, e, d, half))
                    pending.append(copy)
        return halves

    def gather_relay(n, view, halves):
        copies = []
        for copy, h, e, d, half in halves:
            if half != e:
                copies.append(copy)
                continue
            copy.wait_recv()
            pair = pl.ds(2 * half, 2)
            if h == 0:
                part, device = view(0, (z - d + 4) % 4, pair), (r, 4 * ((z + d) % 4) + y)
            else:
                part, device = view(1, pair, (y - d + 4) % 4), (r, 4 * z + (y + d) % 4)
            s = 14 + 2 * h + e
            relayed = send("gather", part, part, g_send.at[n, s], g_recv.at[n, s], device)
            copies.append(relayed)
            pending.append(relayed)
        return copies

    def wait_all(copies):
        for copy in copies:
            copy.wait_recv()

    def slab_view(buf):
        return lambda h, zz, yy: buf.at[zz, yy, pl.ds(64 * h, 64)]

    def diag_view(p):
        width = 256 * (p + 1)
        return lambda h, zz, yy: dm.at[p, k, zz, yy, :, pl.ds(width * h, width)]

    back_slot = 2 * back_x + k
    ahead_slot = 2 * ahead_x + k
    far_slot = 2 * far_x + k

    def panel_copy(kind, t, j):
        if t == 0:
            slot = {PASS_AHEAD: back_slot, BACK_SIB: back_slot, AHEAD_SIB: ahead_slot, FAR_SIB: far_slot}.get(kind, r)
            src = dst = cr.at[j, slot]
        else:
            here = {PASS_AHEAD: 2 - k, BACK_SIB: 2 - k, AHEAD_SIB: 1 + k, FAR_SIB: 3}.get(kind, 0)
            there = {OWN_AHEAD: 2 - k, OWN_BACK: 1 + k, PASS_AHEAD: 3}.get(kind, here)
            src, dst = cl.at[j, here, k], cl.at[j, there, k]
        device = {OWN_AHEAD: ahead, PASS_AHEAD: ahead, OWN_BACK: back}.get(kind, sib)
        s = 4 * t + j
        return remote("panel", src, dst, x_send.at[kind, s], x_recv.at[kind, s], device)

    def panel_own(t, j):
        for kind in (OWN_AHEAD, OWN_BACK, OWN_SIB):
            panel_copy(kind, t, j).start()

    def panel_pass(t, j):
        panel_copy(OWN_AHEAD, t, j).wait_recv()
        panel_copy(PASS_AHEAD, t, j).start()
        panel_copy(BACK_SIB, t, j).start()
        panel_copy(OWN_BACK, t, j).wait_recv()
        panel_copy(AHEAD_SIB, t, j).start()

    def panel_far(t, j):
        panel_copy(PASS_AHEAD, t, j).wait_recv()
        panel_copy(FAR_SIB, t, j).start()

    def panel_sibling(t, j, kinds):
        for kind in kinds:
            panel_copy(kind, t, j).wait_recv()

    for p in range(4):

        @pl.when(x == p)
        def _():
            for n, device in enumerate((ahead, back, far)):
                part = pl.ds(0, 512 * (p + 1))
                send("diag", diag.at[:, part], dm.at[p, k, z, y, :, part], d_send.at[n], d_recv.at[p], device)

    x_view, l_view = slab_view(xr), slab_view(rl)
    d_view = [diag_view(p) for p in range(4)]
    x_first = gather_first(0, [row_right.at[0, pl.ds(64 * h, 64)] for h in range(2)], x_view)
    l_first = gather_first(1, [row_left.at[0, pl.ds(64 * h, 64)] for h in range(2)], l_view)
    load_cr.wait()
    load_cl.wait()
    for j in range(4):
        panel_own(0, j)
    for j in range(4):
        panel_own(1, j)

    def local_products(j):
        load_tl[j].wait()
        g = tdot(tl[j], tl[j])
        keep = lax.broadcasted_iota(jnp.int32, (256, 256), 1) < rank_n[0, j]
        gram[j] = jnp.where(keep, g, 0.0).astype(BF16)

    def diag_share(p):
        wait_all(d_relay[p])
        part = dm.at[p, k, :, :, :, pl.ds(0, 512 * (p + 1))]
        copy = send("diag", part, part, a_send.at[p], a_recv.at[p], sib)
        pending.append(copy)
        return copy

    def solve(p, q):
        width = 512 * (p + 1)
        solved = dot(dm[p, q, :, :, :, 0:width].reshape(256, width), xr[0 : p + 1].reshape(width, 256))
        st[p, q] = solved.astype(BF16).T

    def solve_back(p):
        rows = jnp.concatenate([st[m, q] for m in range(p, 4) for q in range(2)], axis=1)
        block = dm[p:4, :, :, :, :, 512 * p : 512 * p + 512].reshape(512 * (4 - p), 512)
        yt[:, 512 * p : 512 * p + 512] = dot(rows, block).astype(BF16)

    chips = (x, (x + 1) % 4, (x + 3) % 4, far_x)

    def chip_rows(i):
        return pl.ds(pl.multiple_of(chips[i] * 512, 512), 512)

    def first_term(j):
        for i in range(4):
            term[j, i] = dot(tr[j, chip_rows(i), :], gram[j])

    for copy in load_ranks:
        copy.wait()
    local_products(0)
    load_x.wait()
    x_second = gather_second(0, x_view, x_first)
    load_d.wait()
    d_first, d_second, d_relay = {}, {}, {}
    for p in (3, 2, 1, 0):

        @pl.when(x != p)
        def _():
            part = dm.at[p, k, z, y, :, pl.ds(0, 512 * (p + 1))]
            remote("diag", part, part, d_send.at[0], d_recv.at[p], far).wait_recv()

        d_first[p] = gather_first(2 + p, [d_view[p](h, z, y) for h in range(2)], d_view[p])
    local_products(1)
    panel_pass(0, 0)
    local_products(2)
    x_relay = gather_relay(0, x_view, x_second)
    for p in (3, 2, 1, 0):
        d_second[p] = gather_second(2 + p, d_view[p], d_first[p])
    panel_pass(0, 1)
    local_products(3)
    load_tr.wait()
    first_term(0)
    panel_pass(0, 2)
    first_term(1)
    first_term(2)
    panel_pass(0, 3)
    first_term(3)
    wait_all(x_relay)
    for p in (3, 2, 1, 0):
        d_relay[p] = gather_relay(2 + p, d_view[p], d_second[p])
    panel_pass(1, 0)
    shares = {3: diag_share(3)}
    solve(3, k)
    panel_pass(1, 1)
    shares[2] = diag_share(2)
    load_l.wait()
    l_second = gather_second(1, l_view, l_first)
    solve(2, k)
    panel_pass(1, 2)
    shares.update({p: diag_share(p) for p in (1, 0)})
    for p in (3, 2):
        shares[p].wait_recv()
        solve(p, 1 - k)
        solve_back(p)
    panel_pass(1, 3)
    l_relay = gather_relay(1, l_view, l_second)
    for p in (1, 0):
        solve(p, k)
        shares[p].wait_recv()
        solve(p, 1 - k)
        solve_back(p)
    for j in range(4):
        panel_far(0, j)

    for j in range(4):
        panel_sibling(0, j, (OWN_SIB, BACK_SIB, AHEAD_SIB, FAR_SIB))
        g = dot(yt[...], cr[j].reshape(2048, 256))
        keep = (lax.broadcasted_iota(jnp.int32, (256, 256), 0) < row_ranks[0]) & (
            lax.broadcasted_iota(jnp.int32, (256, 256), 1) < rank_c[j]
        )
        coup[j] = jnp.where(keep, g, 0.0).astype(BF16).T
    wait_all(l_relay)
    for j in range(4):
        projected = tdot(rl[...].reshape(2048, 256), tl[j]).astype(BF16)
        cm = dot(coup[j], projected)
        keep = lax.broadcasted_iota(jnp.int32, (256, 256), 1) < rank_n[0, j]
        comb[j] = jnp.where(keep, cm, 0.0).astype(BF16)

    def update(i, j):
        second = dot(cl[j, i].reshape(512, 256), comb[j])
        out[0, j, chip_rows(i), :] = (term[j, i] - second).astype(BF16)

    for j in range(4):
        panel_far(1, j)
        panel_sibling(1, j, (OWN_SIB, BACK_SIB, AHEAD_SIB))
        for i in range(3):
            update(i, j)
    for j in range(4):
        panel_sibling(1, j, (FAR_SIB,))
        update(3, j)

    for p in range(4):

        @pl.when(x == p)
        def _():
            for n in range(3):
                part = dm.at[p, k, z, y, :, pl.ds(0, 512 * (p + 1))]
                remote("diag", part, part, d_send.at[n], d_recv.at[p], far).wait_send()

    for copy in pending:
        copy.wait_send()
    for t in range(2):
        for j in range(4):
            for kind in range(7):
                panel_copy(kind, t, j).wait_send()


def on_device(
    diag_inverse, row_left, row_right, col_left, col_right, row_ranks, col_ranks, tile_left, tile_right, new_ranks
):
    hbm = pl.BlockSpec(memory_space=pltpu.HBM)
    operands = (
        col_ranks, new_ranks, diag_inverse, row_left, row_right, col_left, col_right, tile_left, tile_right
    )
    dma = pltpu.SemaphoreType.DMA
    return pl.pallas_call(
        kernel,
        out_shape=pltpu.VMEM(tile_right.shape, tile_right.dtype),
        in_specs=[pl.BlockSpec(memory_space=pltpu.SMEM)] + [hbm] * 9,
        out_specs=pl.BlockSpec(memory_space=pltpu.VMEM),
        scratch_shapes=[
            pltpu.VMEM((4, 2048, 256), BF16),
            pltpu.VMEM((4, 2048, 256), BF16),
            pltpu.VMEM((4, 8, 256, 256), BF16),
            pltpu.VMEM((4, 4, 2, 256, 256), BF16),
            pltpu.VMEM((4, 4, 128, 256), BF16),
            pltpu.VMEM((4, 4, 128, 256), BF16),
            pltpu.VMEM((4, 2, 256, 256), BF16),
            pltpu.VMEM((256, 2048), BF16),
            pltpu.VMEM((4, 2, 4, 4, 16, 2048), BF16),
            pltpu.VMEM((4, 256, 256), BF16),
            pltpu.VMEM((4, 256, 256), BF16),
            pltpu.VMEM((4, 256, 256), BF16),
            pltpu.VMEM((4, 4, 512, 256), F32),
            pltpu.SMEM((4,), jnp.int32),
            pltpu.SMEM((1, 4), jnp.int32),
            dma((12,)),
            dma((7, 8)),
            dma((7, 8)),
            dma((3,)),
            dma((4,)),
            dma((4,)),
            dma((4,)),
            dma((6, 18)),
            dma((6, 18)),
        ],
        compiler_params=pltpu.CompilerParams(
            collective_id=0, has_side_effects=True, vmem_limit_bytes=52 * 1024 * 1024
        ),
        name="panel_step",
    )(row_ranks, *[pltpu.with_memory_space_constraint(a, pltpu.HBM) for a in operands])


def solution(mesh):
    in_specs = (
        P(("row", "col"), None),
        P("row", "col", None),
        P("row", "col", None),
        P("col", "row", None),
        P("col", "row", None),
        P("row"),
        P("col"),
        P("row", "col", None, None),
        P("row", "col", None, None),
        P("row", "col"),
    )
    out_specs = P("row", "col", None, None)
    return jax.shard_map(on_device, mesh=mesh, in_specs=in_specs, out_specs=out_specs, check_vma=False)
```

```python
import functools

import jax
import jax.numpy as jnp
from jax import lax
from jax.experimental import pallas as pl
from jax.experimental.pallas import tpu as pltpu
from jax.sharding import PartitionSpec as P

MESH = pl.DeviceIdType.MESH
F32 = jnp.float32
BF16 = jnp.bfloat16

OWN_AHEAD, OWN_BACK, OWN_SIB, PASS_AHEAD, BACK_SIB, AHEAD_SIB, FAR_SIB = range(7)


def dot(a, b):
    return jnp.dot(a, b, preferred_element_type=F32)


def tdot(a, b):
    return lax.dot_general(a, b, (((0,), (0,)), ((), ())), preferred_element_type=F32)


def remote(group, src, dst, ssem, rsem, device):
    return pltpu.make_async_remote_copy(
        src_ref=src, dst_ref=dst, send_sem=ssem, recv_sem=rsem, device_id=device, device_id_type=MESH
    )


def kernel(
    row_ranks,
    col_ranks,
    new_ranks,
    diag,
    row_left,
    row_right,
    col_left,
    col_right,
    tile_left,
    tile_right,
    out,
    tl,
    tr,
    cr,
    cl,
    rl,
    xr,
    st,
    yt,
    dm,
    gram,
    proj,
    comb,
    term,
    rank_c,
    rank_n,
    load_sem,
    x_send,
    x_recv,
    d_send,
    d_recv,
    a_send,
    a_recv,
    g_send,
    g_recv,
):
    r = lax.axis_index("row")
    c = lax.axis_index("col")
    x, k = r // 2, r % 2
    z, y = c // 4, c % 4
    step = 1 - 2 * k
    ahead_x = (x + step + 4) % 4
    back_x = (x - step + 4) % 4
    far_x = (x + 2) % 4
    sib = (2 * x + 1 - k, c)
    ahead = (2 * ahead_x + k, c)
    back = (2 * back_x + k, c)
    far = (2 * far_x + k, c)
    pending = []

    def send(group, src, dst, ssem, rsem, device):
        copy = remote(group, src, dst, ssem, rsem, device)
        copy.start()
        return copy

    barrier = pltpu.get_barrier_semaphore()
    for device in (ahead, back, far, sib):
        pl.semaphore_signal(barrier, inc=1, device_id=device, device_id_type=MESH)
    for d in range(1, 4):
        for device in ((r, 4 * z + (y + d) % 4), (r, 4 * ((z + d) % 4) + y)):
            pl.semaphore_signal(barrier, inc=1, device_id=device, device_id_type=MESH)

    def load(src, dst, n):
        copy = pltpu.make_async_copy(src, dst, load_sem.at[n])
        copy.start()
        return copy

    load_ranks = [load(col_ranks, rank_c, 10), load(new_ranks, rank_n, 11)]
    load_x = load(row_right.at[0], xr.at[z, y], 1)
    load_d = load(diag, dm.at[x, k, z, y], 0)
    load_tl = [load(tile_left.at[0, j], tl.at[j], 3 + j) for j in range(4)]
    load_l = load(row_left.at[0], rl.at[z, y], 2)
    load_cr = load(col_right, cr.at[:, r], 7)
    load_cl = load(col_left, cl.at[:, 0, k], 8)
    load_tr = load(tile_right.at[0], tr, 9)
    pl.semaphore_wait(barrier, 10)

    def gather_first(n, sources, view):
        copies = []
        for d in range(1, 4):
            for h, device in ((0, (r, 4 * z + (y + d) % 4)), (1, (r, 4 * ((z + d) % 4) + y))):
                s = 3 * h + d - 1
                copies.append(send("gather", sources[h], view(h, z, y), g_send.at[n, s], g_recv.at[n, s], device))
        pending.extend(copies)
        return copies

    def gather_second(n, view, firsts):
        wait_all(firsts)
        halves = []
        for e, d in ((0, 1), (1, 3)):
            for half in (e, 1 - e):
                pair = pl.ds(2 * half, 2)
                for h, device in ((0, (r, 4 * ((z + d) % 4) + y)), (1, (r, 4 * z + (y + d) % 4))):
                    part = view(0, z, pair) if h == 0 else view(1, pair, y)
                    s = 6 + 4 * h + 2 * e + half
                    copy = send("gather", part, part, g_send.at[n, s], g_recv.at[n, s], device)
                    halves.append((copy, h, e, d, half))
                    pending.append(copy)
        return halves

    def gather_direct(n, view, firsts):
        wait_all(firsts)
        copies = []
        for d in (1, 3, 2):
            for h, device in ((0, (r, 4 * ((z + d) % 4) + y)), (1, (r, 4 * z + (y + d) % 4))):
                part = view(0, z, slice(None)) if h == 0 else view(1, slice(None), y)
                s = 6 + 3 * h + d - 1
                copies.append(send("gather", part, part, g_send.at[n, s], g_recv.at[n, s], device))
        pending.extend(copies)
        return copies

    def gather_relay(n, view, halves):
        copies = []
        for copy, h, e, d, half in halves:
            if half != e:
                copies.append(copy)
                continue
            copy.wait_recv()
            pair = pl.ds(2 * half, 2)
            if h == 0:
                part, device = view(0, (z - d + 4) % 4, pair), (r, 4 * ((z + d) % 4) + y)
            else:
                part, device = view(1, pair, (y - d + 4) % 4), (r, 4 * z + (y + d) % 4)
            s = 14 + 2 * h + e
            relayed = send("gather", part, part, g_send.at[n, s], g_recv.at[n, s], device)
            copies.append(relayed)
            pending.append(relayed)
        return copies

    def wait_all(copies):
        for copy in copies:
            copy.wait_recv()

    def slab_view(buf):
        return lambda h, zz, yy: buf.at[zz, yy, pl.ds(64 * h, 64)]

    def diag_view(p):
        width = 256 * (p + 1)
        return lambda h, zz, yy: dm.at[p, k, zz, yy, :, pl.ds(width * h, width)]

    back_slot = 2 * back_x + k
    ahead_slot = 2 * ahead_x + k
    far_slot = 2 * far_x + k

    def panel_copy(kind, t, j):
        if t == 0:
            slot = {PASS_AHEAD: back_slot, BACK_SIB: back_slot, AHEAD_SIB: ahead_slot, FAR_SIB: far_slot}.get(kind, r)
            src = dst = cr.at[j, slot]
        else:
            here = {PASS_AHEAD: 2 - k, BACK_SIB: 2 - k, AHEAD_SIB: 1 + k, FAR_SIB: 3}.get(kind, 0)
            there = {OWN_AHEAD: 2 - k, OWN_BACK: 1 + k, PASS_AHEAD: 3}.get(kind, here)
            src, dst = cl.at[j, here, k], cl.at[j, there, k]
        device = {OWN_AHEAD: ahead, PASS_AHEAD: ahead, OWN_BACK: back}.get(kind, sib)
        s = 4 * t + j
        return remote("panel", src, dst, x_send.at[kind, s], x_recv.at[kind, s], device)

    def panel_own(t, j):
        for kind in (OWN_AHEAD, OWN_BACK, OWN_SIB):
            panel_copy(kind, t, j).start()

    def panel_pass(t, j):
        panel_copy(OWN_AHEAD, t, j).wait_recv()
        panel_copy(PASS_AHEAD, t, j).start()
        panel_copy(BACK_SIB, t, j).start()
        panel_copy(OWN_BACK, t, j).wait_recv()
        panel_copy(AHEAD_SIB, t, j).start()

    def panel_far(t, j):
        panel_copy(PASS_AHEAD, t, j).wait_recv()
        panel_copy(FAR_SIB, t, j).start()

    def panel_sibling(t, j, kinds):
        for kind in kinds:
            panel_copy(kind, t, j).wait_recv()

    for p in range(4):

        @pl.when(x == p)
        def _():
            for n, device in enumerate((ahead, back, far)):
                part = pl.ds(0, 512 * (p + 1))
                send("diag", diag.at[:, part], dm.at[p, k, z, y, :, part], d_send.at[n], d_recv.at[p], device)

    x_view, l_view = slab_view(xr), slab_view(rl)
    d_view = [diag_view(p) for p in range(4)]
    x_first = gather_first(0, [row_right.at[0, pl.ds(64 * h, 64)] for h in range(2)], x_view)
    l_first = gather_first(1, [row_left.at[0, pl.ds(64 * h, 64)] for h in range(2)], l_view)
    load_cr.wait()
    load_cl.wait()
    for j in range(4):
        panel_own(0, j)
    for j in range(4):
        panel_own(1, j)

    def local_products(j):
        load_tl[j].wait()
        g = tdot(tl[j], tl[j])
        keep = lax.broadcasted_iota(jnp.int32, (256, 256), 1) < rank_n[0, j]
        gram[j] = jnp.where(keep, g, 0.0).astype(BF16)

    def diag_share(p):
        wait_all(d_relay[p])
        part = dm.at[p, k, :, :, :, pl.ds(0, 512 * (p + 1))]
        copy = send("diag", part, part, a_send.at[p], a_recv.at[p], sib)
        pending.append(copy)
        return copy

    def solve(p, q):
        width = 512 * (p + 1)
        solved = dot(dm[p, q, :, :, :, 0:width].reshape(256, width), xr[0 : p + 1].reshape(width, 256))
        st[p, q] = solved.astype(BF16).T

    def solve_both(p):
        width = 512 * (p + 1)
        solved = dot(dm[p, :, :, :, :, 0:width].reshape(512, width), xr[0 : p + 1].reshape(width, 256))
        solved = solved.astype(BF16)
        for q in range(2):
            st[p, q] = solved[256 * q : 256 * q + 256].T

    def solve_back(p):
        rows = jnp.concatenate([st[m, q] for m in range(p, 4) for q in range(2)], axis=1)
        block = dm[p:4, :, :, :, :, 512 * p : 512 * p + 512].reshape(512 * (4 - p), 512)
        yt[:, 512 * p : 512 * p + 512] = dot(rows, block).astype(BF16)

    chips = (x, (x + 1) % 4, (x + 3) % 4, far_x)

    def chip_rows(i):
        return pl.ds(pl.multiple_of(chips[i] * 512, 512), 512)

    def first_term(j):
        for i in range(4):
            term[j, i] = dot(tr[j, chip_rows(i), :], gram[j])

    for copy in load_ranks:
        copy.wait()
    local_products(0)
    load_x.wait()
    x_second = gather_second(0, x_view, x_first)
    load_d.wait()
    d_first, d_second, d_relay = {}, {}, {}
    for p in (3, 2, 1, 0):

        @pl.when(x != p)
        def _():
            part = dm.at[p, k, z, y, :, pl.ds(0, 512 * (p + 1))]
            remote("diag", part, part, d_send.at[0], d_recv.at[p], far).wait_recv()

        d_first[p] = gather_first(2 + p, [d_view[p](h, z, y) for h in range(2)], d_view[p])
    local_products(1)
    panel_pass(0, 0)
    local_products(2)
    x_relay = gather_relay(0, x_view, x_second)
    for p in (3, 2, 1, 0):
        d_second[p] = gather_second(2 + p, d_view[p], d_first[p])
    panel_pass(0, 1)
    local_products(3)
    load_tr.wait()
    first_term(0)
    panel_pass(0, 2)
    first_term(1)
    first_term(2)
    panel_pass(0, 3)
    first_term(3)
    wait_all(x_relay)
    for p in (3, 2, 1, 0):
        d_relay[p] = gather_relay(2 + p, d_view[p], d_second[p])
    load_l.wait()
    l_second = gather_direct(1, l_view, l_first)
    panel_pass(1, 0)
    shares = {3: diag_share(3)}
    solve(3, k)
    panel_pass(1, 1)
    shares[2] = diag_share(2)
    solve(2, k)
    panel_pass(1, 2)
    shares.update({p: diag_share(p) for p in (1, 0)})
    for p in (3, 2):
        shares[p].wait_recv()
        solve(p, 1 - k)
        solve_back(p)
    panel_pass(1, 3)
    for p in (1, 0):
        shares[p].wait_recv()
        solve_both(p)
        solve_back(p)
    panel_far(0, 0)

    wait_all(l_second)
    for j in range(4):
        proj[j] = tdot(rl[...].reshape(2048, 256), tl[j]).astype(BF16)
        if j < 3:
            panel_far(0, j + 1)
    for j in range(4):
        panel_sibling(0, j, (OWN_SIB, BACK_SIB, AHEAD_SIB, FAR_SIB))
        g = dot(yt[...], cr[j].reshape(2048, 256))
        keep = (lax.broadcasted_iota(jnp.int32, (256, 256), 0) < row_ranks[0]) & (
            lax.broadcasted_iota(jnp.int32, (256, 256), 1) < rank_c[j]
        )
        coupling = jnp.where(keep, g, 0.0).astype(BF16)
        cm = tdot(coupling, proj[j])
        keep = lax.broadcasted_iota(jnp.int32, (256, 256), 1) < rank_n[0, j]
        comb[j] = jnp.where(keep, cm, 0.0).astype(BF16)

    def update(i, j):
        second = dot(cl[j, i].reshape(512, 256), comb[j])
        out[0, j, chip_rows(i), :] = (term[j, i] - second).astype(BF16)

    for j in range(4):
        panel_far(1, j)
        panel_sibling(1, j, (OWN_SIB, BACK_SIB, AHEAD_SIB))
        for i in range(3):
            update(i, j)
    for j in range(4):
        panel_sibling(1, j, (FAR_SIB,))
        update(3, j)

    for p in range(4):

        @pl.when(x == p)
        def _():
            for n in range(3):
                part = dm.at[p, k, z, y, :, pl.ds(0, 512 * (p + 1))]
                remote("diag", part, part, d_send.at[n], d_recv.at[p], far).wait_send()

    for copy in pending:
        copy.wait_send()
    for t in range(2):
        for j in range(4):
            for kind in range(7):
                panel_copy(kind, t, j).wait_send()


def on_device(
    diag_inverse, row_left, row_right, col_left, col_right, row_ranks, col_ranks, tile_left, tile_right, new_ranks
):
    hbm = pl.BlockSpec(memory_space=pltpu.HBM)
    operands = (
        col_ranks, new_ranks, diag_inverse, row_left, row_right, col_left, col_right, tile_left, tile_right
    )
    dma = pltpu.SemaphoreType.DMA
    return pl.pallas_call(
        kernel,
        out_shape=pltpu.VMEM(tile_right.shape, tile_right.dtype),
        in_specs=[pl.BlockSpec(memory_space=pltpu.SMEM)] + [hbm] * 9,
        out_specs=pl.BlockSpec(memory_space=pltpu.VMEM),
        scratch_shapes=[
            pltpu.VMEM((4, 2048, 256), BF16),
            pltpu.VMEM((4, 2048, 256), BF16),
            pltpu.VMEM((4, 8, 256, 256), BF16),
            pltpu.VMEM((4, 4, 2, 256, 256), BF16),
            pltpu.VMEM((4, 4, 128, 256), BF16),
            pltpu.VMEM((4, 4, 128, 256), BF16),
            pltpu.VMEM((4, 2, 256, 256), BF16),
            pltpu.VMEM((256, 2048), BF16),
            pltpu.VMEM((4, 2, 4, 4, 16, 2048), BF16),
            pltpu.VMEM((4, 256, 256), BF16),
            pltpu.VMEM((4, 256, 256), BF16),
            pltpu.VMEM((4, 256, 256), BF16),
            pltpu.VMEM((4, 4, 512, 256), F32),
            pltpu.SMEM((4,), jnp.int32),
            pltpu.SMEM((1, 4), jnp.int32),
            dma((12,)),
            dma((7, 8)),
            dma((7, 8)),
            dma((3,)),
            dma((4,)),
            dma((4,)),
            dma((4,)),
            dma((6, 18)),
            dma((6, 18)),
        ],
        compiler_params=pltpu.CompilerParams(
            collective_id=0, has_side_effects=True, vmem_limit_bytes=52 * 1024 * 1024
        ),
        name="panel_step",
    )(row_ranks, *[pltpu.with_memory_space_constraint(a, pltpu.HBM) for a in operands])


def solution(mesh):
    in_specs = (
        P(("row", "col"), None),
        P("row", "col", None),
        P("row", "col", None),
        P("col", "row", None),
        P("col", "row", None),
        P("row"),
        P("col"),
        P("row", "col", None, None),
        P("row", "col", None, None),
        P("row", "col"),
    )
    out_specs = P("row", "col", None, None)
    return jax.shard_map(on_device, mesh=mesh, in_specs=in_specs, out_specs=out_specs, check_vma=False)
```

```python
import functools

import jax
import jax.numpy as jnp
from jax import lax
from jax.experimental import pallas as pl
from jax.experimental.pallas import tpu as pltpu
from jax.sharding import PartitionSpec as P

MESH = pl.DeviceIdType.MESH
F32 = jnp.float32
BF16 = jnp.bfloat16

OWN_AHEAD, OWN_BACK, OWN_SIB, PASS_AHEAD, BACK_SIB, AHEAD_SIB, FAR_SIB = range(7)


def dot(a, b):
    return jnp.dot(a, b, preferred_element_type=F32)


def tdot(a, b):
    return lax.dot_general(a, b, (((0,), (0,)), ((), ())), preferred_element_type=F32)


def remote(group, src, dst, ssem, rsem, device):
    return pltpu.make_async_remote_copy(
        src_ref=src, dst_ref=dst, send_sem=ssem, recv_sem=rsem, device_id=device, device_id_type=MESH
    )


def kernel(
    row_ranks,
    col_ranks,
    new_ranks,
    diag,
    row_left,
    row_right,
    col_left,
    col_right,
    tile_left,
    tile_right,
    out,
    tl,
    tr,
    cr,
    cl,
    rl,
    xr,
    st,
    yt,
    dm,
    gram,
    proj,
    comb,
    term,
    rank_c,
    rank_n,
    load_sem,
    x_send,
    x_recv,
    d_send,
    d_recv,
    a_send,
    a_recv,
    g_send,
    g_recv,
):
    r = lax.axis_index("row")
    c = lax.axis_index("col")
    x, k = r // 2, r % 2
    z, y = c // 4, c % 4
    step = 1 - 2 * k
    ahead_x = (x + step + 4) % 4
    back_x = (x - step + 4) % 4
    far_x = (x + 2) % 4
    sib = (2 * x + 1 - k, c)
    ahead = (2 * ahead_x + k, c)
    back = (2 * back_x + k, c)
    far = (2 * far_x + k, c)
    pending = []

    def send(group, src, dst, ssem, rsem, device):
        copy = remote(group, src, dst, ssem, rsem, device)
        copy.start()
        return copy

    barrier = pltpu.get_barrier_semaphore()
    for device in (ahead, back, far, sib):
        pl.semaphore_signal(barrier, inc=1, device_id=device, device_id_type=MESH)
    for d in range(1, 4):
        for device in ((r, 4 * z + (y + d) % 4), (r, 4 * ((z + d) % 4) + y)):
            pl.semaphore_signal(barrier, inc=1, device_id=device, device_id_type=MESH)

    def load(src, dst, n):
        copy = pltpu.make_async_copy(src, dst, load_sem.at[n])
        copy.start()
        return copy

    load_ranks = [load(col_ranks, rank_c, 10), load(new_ranks, rank_n, 11)]
    load_x = load(row_right.at[0], xr.at[z, y], 1)
    load_d = load(diag, dm.at[x, k, z, y], 0)
    load_tl = [load(tile_left.at[0, j], tl.at[j], 3 + j) for j in range(4)]
    load_l = load(row_left.at[0], rl.at[z, y], 2)
    load_cr = load(col_right, cr.at[:, r], 7)
    load_cl = load(col_left, cl.at[:, 0, k], 8)
    load_tr = load(tile_right.at[0], tr, 9)
    pl.semaphore_wait(barrier, 10)

    def gather_first(n, sources, view):
        copies = []
        for d in range(1, 4):
            for h, device in ((0, (r, 4 * z + (y + d) % 4)), (1, (r, 4 * ((z + d) % 4) + y))):
                s = 3 * h + d - 1
                copies.append(send("gather", sources[h], view(h, z, y), g_send.at[n, s], g_recv.at[n, s], device))
        pending.extend(copies)
        return copies

    def gather_second(n, view, firsts):
        wait_all(firsts)
        halves = []
        for e, d in ((0, 1), (1, 3)):
            for half in (e, 1 - e):
                pair = pl.ds(2 * half, 2)
                for h, device in ((0, (r, 4 * ((z + d) % 4) + y)), (1, (r, 4 * z + (y + d) % 4))):
                    part = view(0, z, pair) if h == 0 else view(1, pair, y)
                    s = 6 + 4 * h + 2 * e + half
                    copy = send("gather", part, part, g_send.at[n, s], g_recv.at[n, s], device)
                    halves.append((copy, h, e, d, half))
                    pending.append(copy)
        return halves

    def gather_direct(n, view, firsts):
        wait_all(firsts)
        copies = []
        for d in (1, 3, 2):
            for h, device in ((0, (r, 4 * ((z + d) % 4) + y)), (1, (r, 4 * z + (y + d) % 4))):
                part = view(0, z, slice(None)) if h == 0 else view(1, slice(None), y)
                s = 6 + 3 * h + d - 1
                copies.append(send("gather", part, part, g_send.at[n, s], g_recv.at[n, s], device))
        pending.extend(copies)
        return copies

    def gather_relay(n, view, halves):
        copies = []
        for copy, h, e, d, half in halves:
            if half != e:
                copies.append(copy)
                continue
            copy.wait_recv()
            pair = pl.ds(2 * half, 2)
            if h == 0:
                part, device = view(0, (z - d + 4) % 4, pair), (r, 4 * ((z + d) % 4) + y)
            else:
                part, device = view(1, pair, (y - d + 4) % 4), (r, 4 * z + (y + d) % 4)
            s = 14 + 2 * h + e
            relayed = send("gather", part, part, g_send.at[n, s], g_recv.at[n, s], device)
            copies.append(relayed)
            pending.append(relayed)
        return copies

    def wait_all(copies):
        for copy in copies:
            copy.wait_recv()

    def slab_view(buf):
        return lambda h, zz, yy: buf.at[zz, yy, pl.ds(64 * h, 64)]

    def diag_view(p):
        width = 256 * (p + 1)
        return lambda h, zz, yy: dm.at[p, k, zz, yy, :, pl.ds(width * h, width)]

    back_slot = 2 * back_x + k
    ahead_slot = 2 * ahead_x + k
    far_slot = 2 * far_x + k

    def panel_copy(kind, t, j):
        if t == 0:
            slot = {PASS_AHEAD: back_slot, BACK_SIB: back_slot, AHEAD_SIB: ahead_slot, FAR_SIB: far_slot}.get(kind, r)
            src = dst = cr.at[j, slot]
        else:
            here = {PASS_AHEAD: 2 - k, BACK_SIB: 2 - k, AHEAD_SIB: 1 + k, FAR_SIB: 3}.get(kind, 0)
            there = {OWN_AHEAD: 2 - k, OWN_BACK: 1 + k, PASS_AHEAD: 3}.get(kind, here)
            src, dst = cl.at[j, here, k], cl.at[j, there, k]
        device = {OWN_AHEAD: ahead, PASS_AHEAD: ahead, OWN_BACK: back}.get(kind, sib)
        s = 4 * t + j
        return remote("panel", src, dst, x_send.at[kind, s], x_recv.at[kind, s], device)

    def panel_own(t, j):
        for kind in (OWN_AHEAD, OWN_BACK, OWN_SIB):
            panel_copy(kind, t, j).start()

    def panel_pass(t, j):
        panel_copy(OWN_AHEAD, t, j).wait_recv()
        panel_copy(PASS_AHEAD, t, j).start()
        panel_copy(BACK_SIB, t, j).start()
        panel_copy(OWN_BACK, t, j).wait_recv()
        panel_copy(AHEAD_SIB, t, j).start()

    def panel_far(t, j):
        panel_copy(PASS_AHEAD, t, j).wait_recv()
        panel_copy(FAR_SIB, t, j).start()

    def panel_sibling(t, j, kinds):
        for kind in kinds:
            panel_copy(kind, t, j).wait_recv()

    for p in range(4):

        @pl.when(x == p)
        def _():
            for n, device in enumerate((ahead, back, far)):
                part = pl.ds(0, 512 * (p + 1))
                send("diag", diag.at[:, part], dm.at[p, k, z, y, :, part], d_send.at[n], d_recv.at[p], device)

    x_view, l_view = slab_view(xr), slab_view(rl)
    d_view = [diag_view(p) for p in range(4)]
    x_first = gather_first(0, [row_right.at[0, pl.ds(64 * h, 64)] for h in range(2)], x_view)
    l_first = gather_first(1, [row_left.at[0, pl.ds(64 * h, 64)] for h in range(2)], l_view)
    load_cr.wait()
    load_cl.wait()
    for j in range(4):
        panel_own(0, j)
    for j in range(4):
        panel_own(1, j)

    def local_products(j):
        load_tl[j].wait()
        g = tdot(tl[j], tl[j])
        keep = lax.broadcasted_iota(jnp.int32, (256, 256), 1) < rank_n[0, j]
        gram[j] = jnp.where(keep, g, 0.0).astype(BF16)

    def diag_share(p):
        wait_all(d_relay[p])
        part = dm.at[p, k, :, :, :, pl.ds(0, 512 * (p + 1))]
        copy = send("diag", part, part, a_send.at[p], a_recv.at[p], sib)
        pending.append(copy)
        return copy

    def solve(p, q):
        width = 512 * (p + 1)
        solved = dot(dm[p, q, :, :, :, 0:width].reshape(256, width), xr[0 : p + 1].reshape(width, 256))
        st[p, q] = solved.astype(BF16).T

    def solve_both(p):
        width = 512 * (p + 1)
        solved = dot(dm[p, :, :, :, :, 0:width].reshape(512, width), xr[0 : p + 1].reshape(width, 256))
        solved = solved.astype(BF16)
        for q in range(2):
            st[p, q] = solved[256 * q : 256 * q + 256].T

    def solve_back(p):
        rows = jnp.concatenate([st[m, q] for m in range(p, 4) for q in range(2)], axis=1)
        block = dm[p:4, :, :, :, :, 512 * p : 512 * p + 512].reshape(512 * (4 - p), 512)
        yt[:, 512 * p : 512 * p + 512] = dot(rows, block).astype(BF16)

    chips = (x, (x + 1) % 4, (x + 3) % 4, far_x)

    def chip_rows(i):
        return pl.ds(pl.multiple_of(chips[i] * 512, 512), 512)

    def first_term(j):
        for i in range(4):
            term[j, i] = dot(tr[j, chip_rows(i), :], gram[j])

    for copy in load_ranks:
        copy.wait()
    local_products(0)
    load_x.wait()
    x_second = gather_second(0, x_view, x_first)
    load_d.wait()
    d_first, d_second, d_relay = {}, {}, {}
    for p in (3, 2, 1, 0):

        @pl.when(x != p)
        def _():
            part = dm.at[p, k, z, y, :, pl.ds(0, 512 * (p + 1))]
            remote("diag", part, part, d_send.at[0], d_recv.at[p], far).wait_recv()

        d_first[p] = gather_first(2 + p, [d_view[p](h, z, y) for h in range(2)], d_view[p])
    local_products(1)
    panel_pass(0, 0)
    local_products(2)
    x_relay = gather_relay(0, x_view, x_second)
    for p in (3, 2, 1, 0):
        d_second[p] = gather_second(2 + p, d_view[p], d_first[p])
    panel_pass(0, 1)
    local_products(3)
    load_tr.wait()
    first_term(0)
    panel_pass(0, 2)
    first_term(1)
    first_term(2)
    panel_pass(0, 3)
    first_term(3)
    wait_all(x_relay)
    for p in (3, 2, 1, 0):
        d_relay[p] = gather_relay(2 + p, d_view[p], d_second[p])
    load_l.wait()
    l_second = gather_direct(1, l_view, l_first)
    panel_pass(1, 0)
    shares = {3: diag_share(3)}
    solve(3, k)
    shares[2] = diag_share(2)
    solve(2, k)
    panel_pass(1, 1)
    shares.update({p: diag_share(p) for p in (1, 0)})
    for p in (3, 2):
        shares[p].wait_recv()
        solve(p, 1 - k)
        solve_back(p)
        panel_pass(1, 5 - p)
    for p in (1, 0):
        shares[p].wait_recv()
        solve_both(p)
        solve_back(p)

    wait_all(l_second)
    for j in range(4):
        proj[j] = tdot(rl[...].reshape(2048, 256), tl[j]).astype(BF16)
        panel_far(0, j)
    for j in range(4):
        panel_sibling(0, j, (OWN_SIB, BACK_SIB, AHEAD_SIB, FAR_SIB))
        g = dot(yt[...], cr[j].reshape(2048, 256))
        keep = (lax.broadcasted_iota(jnp.int32, (256, 256), 0) < row_ranks[0]) & (
            lax.broadcasted_iota(jnp.int32, (256, 256), 1) < rank_c[j]
        )
        coupling = jnp.where(keep, g, 0.0).astype(BF16)
        cm = tdot(coupling, proj[j])
        keep = lax.broadcasted_iota(jnp.int32, (256, 256), 1) < rank_n[0, j]
        comb[j] = jnp.where(keep, cm, 0.0).astype(BF16)

    def update(i, j):
        second = dot(cl[j, i].reshape(512, 256), comb[j])
        out[0, j, chip_rows(i), :] = (term[j, i] - second).astype(BF16)

    for j in range(4):
        panel_far(1, j)
        panel_sibling(1, j, (OWN_SIB, BACK_SIB, AHEAD_SIB))
        for i in range(3):
            update(i, j)
    for j in range(4):
        panel_sibling(1, j, (FAR_SIB,))
        update(3, j)

    for p in range(4):

        @pl.when(x == p)
        def _():
            for n in range(3):
                part = dm.at[p, k, z, y, :, pl.ds(0, 512 * (p + 1))]
                remote("diag", part, part, d_send.at[n], d_recv.at[p], far).wait_send()

    for copy in pending:
        copy.wait_send()
    for t in range(2):
        for j in range(4):
            for kind in range(7):
                panel_copy(kind, t, j).wait_send()


def on_device(
    diag_inverse, row_left, row_right, col_left, col_right, row_ranks, col_ranks, tile_left, tile_right, new_ranks
):
    hbm = pl.BlockSpec(memory_space=pltpu.HBM)
    operands = (
        col_ranks, new_ranks, diag_inverse, row_left, row_right, col_left, col_right, tile_left, tile_right
    )
    dma = pltpu.SemaphoreType.DMA
    return pl.pallas_call(
        kernel,
        out_shape=pltpu.VMEM(tile_right.shape, tile_right.dtype),
        in_specs=[pl.BlockSpec(memory_space=pltpu.SMEM)] + [hbm] * 9,
        out_specs=pl.BlockSpec(memory_space=pltpu.VMEM),
        scratch_shapes=[
            pltpu.VMEM((4, 2048, 256), BF16),
            pltpu.VMEM((4, 2048, 256), BF16),
            pltpu.VMEM((4, 8, 256, 256), BF16),
            pltpu.VMEM((4, 4, 2, 256, 256), BF16),
            pltpu.VMEM((4, 4, 128, 256), BF16),
            pltpu.VMEM((4, 4, 128, 256), BF16),
            pltpu.VMEM((4, 2, 256, 256), BF16),
            pltpu.VMEM((256, 2048), BF16),
            pltpu.VMEM((4, 2, 4, 4, 16, 2048), BF16),
            pltpu.VMEM((4, 256, 256), BF16),
            pltpu.VMEM((4, 256, 256), BF16),
            pltpu.VMEM((4, 256, 256), BF16),
            pltpu.VMEM((4, 4, 512, 256), F32),
            pltpu.SMEM((4,), jnp.int32),
            pltpu.SMEM((1, 4), jnp.int32),
            dma((12,)),
            dma((7, 8)),
            dma((7, 8)),
            dma((3,)),
            dma((4,)),
            dma((4,)),
            dma((4,)),
            dma((6, 18)),
            dma((6, 18)),
        ],
        compiler_params=pltpu.CompilerParams(
            collective_id=0, has_side_effects=True, vmem_limit_bytes=52 * 1024 * 1024
        ),
        name="panel_step",
    )(row_ranks, *[pltpu.with_memory_space_constraint(a, pltpu.HBM) for a in operands])


def solution(mesh):
    in_specs = (
        P(("row", "col"), None),
        P("row", "col", None),
        P("row", "col", None),
        P("col", "row", None),
        P("col", "row", None),
        P("row"),
        P("col"),
        P("row", "col", None, None),
        P("row", "col", None, None),
        P("row", "col"),
    )
    out_specs = P("row", "col", None, None)
    return jax.shard_map(on_device, mesh=mesh, in_specs=in_specs, out_specs=out_specs, check_vma=False)
```

```python
import functools

import jax
import jax.numpy as jnp
from jax import lax
from jax.experimental import pallas as pl
from jax.experimental.pallas import tpu as pltpu
from jax.sharding import PartitionSpec as P

MESH = pl.DeviceIdType.MESH
F32 = jnp.float32
BF16 = jnp.bfloat16

OWN_AHEAD, OWN_BACK, OWN_SIB, PASS_AHEAD, BACK_SIB, AHEAD_SIB, FAR_SIB = range(7)


def dot(a, b):
    return jnp.dot(a, b, preferred_element_type=F32)


def tdot(a, b):
    return lax.dot_general(a, b, (((0,), (0,)), ((), ())), preferred_element_type=F32)


def remote(group, src, dst, ssem, rsem, device):
    return pltpu.make_async_remote_copy(
        src_ref=src, dst_ref=dst, send_sem=ssem, recv_sem=rsem, device_id=device, device_id_type=MESH
    )


def kernel(
    row_ranks,
    col_ranks,
    new_ranks,
    diag,
    row_left,
    row_right,
    col_left,
    col_right,
    tile_left,
    tile_right,
    out,
    tl,
    tr,
    cr,
    cl,
    rl,
    xr,
    st,
    yt,
    dm,
    gram,
    proj,
    comb,
    term,
    rank_c,
    rank_n,
    load_sem,
    x_send,
    x_recv,
    d_send,
    d_recv,
    a_send,
    a_recv,
    g_send,
    g_recv,
):
    r = lax.axis_index("row")
    c = lax.axis_index("col")
    x, k = r // 2, r % 2
    z, y = c // 4, c % 4
    step = 1 - 2 * k
    ahead_x = (x + step + 4) % 4
    back_x = (x - step + 4) % 4
    far_x = (x + 2) % 4
    sib = (2 * x + 1 - k, c)
    ahead = (2 * ahead_x + k, c)
    back = (2 * back_x + k, c)
    far = (2 * far_x + k, c)
    pending = []

    def send(group, src, dst, ssem, rsem, device):
        copy = remote(group, src, dst, ssem, rsem, device)
        copy.start()
        return copy

    barrier = pltpu.get_barrier_semaphore()
    for device in (ahead, back, far, sib):
        pl.semaphore_signal(barrier, inc=1, device_id=device, device_id_type=MESH)
    for d in range(1, 4):
        for device in ((r, 4 * z + (y + d) % 4), (r, 4 * ((z + d) % 4) + y)):
            pl.semaphore_signal(barrier, inc=1, device_id=device, device_id_type=MESH)

    def load(src, dst, n):
        copy = pltpu.make_async_copy(src, dst, load_sem.at[n])
        copy.start()
        return copy

    load_x = load(row_right.at[0], xr.at[z, y], 1)
    load_d = load(diag, dm.at[x, k, z, y], 0)
    load_l = load(row_left.at[0], rl.at[z, y], 2)
    load_cr = load(col_right, cr.at[:, r], 7)
    load_cl = load(col_left, cl.at[:, 0, k], 8)
    load_tl = [load(tile_left.at[0, j], tl.at[j], 3 + j) for j in range(4)]
    load_ranks = [load(col_ranks, rank_c, 10), load(new_ranks, rank_n, 11)]
    load_tr = load(tile_right.at[0], tr, 9)
    pl.semaphore_wait(barrier, 10)

    def gather_first(n, sources, view):
        copies = []
        for d in range(1, 4):
            for h, device in ((0, (r, 4 * z + (y + d) % 4)), (1, (r, 4 * ((z + d) % 4) + y))):
                s = 3 * h + d - 1
                copies.append(send("gather", sources[h], view(h, z, y), g_send.at[n, s], g_recv.at[n, s], device))
        pending.extend(copies)
        return copies

    def gather_second(n, view, firsts):
        wait_all(firsts)
        halves = []
        for e, d in ((0, 1), (1, 3)):
            for half in (e, 1 - e):
                pair = pl.ds(2 * half, 2)
                for h, device in ((0, (r, 4 * ((z + d) % 4) + y)), (1, (r, 4 * z + (y + d) % 4))):
                    part = view(0, z, pair) if h == 0 else view(1, pair, y)
                    s = 6 + 4 * h + 2 * e + half
                    copy = send("gather", part, part, g_send.at[n, s], g_recv.at[n, s], device)
                    halves.append((copy, h, e, d, half))
                    pending.append(copy)
        return halves

    def gather_direct(n, view, firsts):
        wait_all(firsts)
        copies = []
        for d in (1, 3, 2):
            for h, device in ((0, (r, 4 * ((z + d) % 4) + y)), (1, (r, 4 * z + (y + d) % 4))):
                part = view(0, z, slice(None)) if h == 0 else view(1, slice(None), y)
                s = 6 + 3 * h + d - 1
                copies.append(send("gather", part, part, g_send.at[n, s], g_recv.at[n, s], device))
        pending.extend(copies)
        return copies

    def gather_relay(n, view, halves):
        copies = []
        for copy, h, e, d, half in halves:
            if half != e:
                copies.append(copy)
                continue
            copy.wait_recv()
            pair = pl.ds(2 * half, 2)
            if h == 0:
                part, device = view(0, (z - d + 4) % 4, pair), (r, 4 * ((z + d) % 4) + y)
            else:
                part, device = view(1, pair, (y - d + 4) % 4), (r, 4 * z + (y + d) % 4)
            s = 14 + 2 * h + e
            relayed = send("gather", part, part, g_send.at[n, s], g_recv.at[n, s], device)
            copies.append(relayed)
            pending.append(relayed)
        return copies

    def wait_all(copies):
        for copy in copies:
            copy.wait_recv()

    def slab_view(buf):
        return lambda h, zz, yy: buf.at[zz, yy, pl.ds(64 * h, 64)]

    def diag_view(p):
        width = 256 * (p + 1)
        return lambda h, zz, yy: dm.at[p, k, zz, yy, :, pl.ds(width * h, width)]

    back_slot = 2 * back_x + k
    ahead_slot = 2 * ahead_x + k
    far_slot = 2 * far_x + k

    def panel_copy(kind, t, j, own=None):
        if t == 0:
            slot = {PASS_AHEAD: back_slot, BACK_SIB: back_slot, AHEAD_SIB: ahead_slot, FAR_SIB: far_slot}.get(kind, r)
            src = dst = cr.at[j, slot]
        else:
            here = {PASS_AHEAD: 2 - k, BACK_SIB: 2 - k, AHEAD_SIB: 1 + k, FAR_SIB: 3}.get(kind, 0)
            there = {OWN_AHEAD: 2 - k, OWN_BACK: 1 + k, PASS_AHEAD: 3}.get(kind, here)
            src, dst = cl.at[j, here, k], cl.at[j, there, k]
        device = {OWN_AHEAD: ahead, PASS_AHEAD: ahead, OWN_BACK: back}.get(kind, sib)
        s = 4 * t + j
        src = src if own is None else own
        return remote("panel", src, dst, x_send.at[kind, s], x_recv.at[kind, s], device)

    sources = (col_right, col_left)

    def panel_own(t, j):
        for kind in (OWN_AHEAD, OWN_BACK, OWN_SIB):
            panel_copy(kind, t, j, sources[t].at[j]).start()

    def panel_pass(t, j):
        panel_copy(OWN_AHEAD, t, j).wait_recv()
        panel_copy(PASS_AHEAD, t, j).start()
        panel_copy(BACK_SIB, t, j).start()
        panel_copy(OWN_BACK, t, j).wait_recv()
        panel_copy(AHEAD_SIB, t, j).start()

    def panel_far(t, j):
        panel_copy(PASS_AHEAD, t, j).wait_recv()
        panel_copy(FAR_SIB, t, j).start()

    def panel_sibling(t, j, kinds):
        for kind in kinds:
            panel_copy(kind, t, j).wait_recv()

    for p in range(4):

        @pl.when(x == p)
        def _():
            for n, device in enumerate((ahead, back, far)):
                part = pl.ds(0, 512 * (p + 1))
                send("diag", diag.at[:, part], dm.at[p, k, z, y, :, part], d_send.at[n], d_recv.at[p], device)

    x_view, l_view = slab_view(xr), slab_view(rl)
    d_view = [diag_view(p) for p in range(4)]
    x_first = gather_first(0, [row_right.at[0, pl.ds(64 * h, 64)] for h in range(2)], x_view)
    l_first = gather_first(1, [row_left.at[0, pl.ds(64 * h, 64)] for h in range(2)], l_view)
    for j in range(4):
        panel_own(0, j)
    for j in range(4):
        panel_own(1, j)

    def local_products(j):
        load_tl[j].wait()
        g = tdot(tl[j], tl[j])
        keep = lax.broadcasted_iota(jnp.int32, (256, 256), 1) < rank_n[0, j]
        gram[j] = jnp.where(keep, g, 0.0).astype(BF16)

    def diag_share(p):
        wait_all(d_relay[p])
        part = dm.at[p, k, :, :, :, pl.ds(0, 512 * (p + 1))]
        copy = send("diag", part, part, a_send.at[p], a_recv.at[p], sib)
        pending.append(copy)
        return copy

    def solve(p, q):
        width = 512 * (p + 1)
        solved = dot(dm[p, q, :, :, :, 0:width].reshape(256, width), xr[0 : p + 1].reshape(width, 256))
        st[p, q] = solved.astype(BF16).T

    def solve_both(p):
        width = 512 * (p + 1)
        solved = dot(dm[p, :, :, :, :, 0:width].reshape(512, width), xr[0 : p + 1].reshape(width, 256))
        solved = solved.astype(BF16)
        for q in range(2):
            st[p, q] = solved[256 * q : 256 * q + 256].T

    def solve_back(p):
        rows = jnp.concatenate([st[m, q] for m in range(p, 4) for q in range(2)], axis=1)
        block = dm[p:4, :, :, :, :, 512 * p : 512 * p + 512].reshape(512 * (4 - p), 512)
        yt[:, 512 * p : 512 * p + 512] = dot(rows, block).astype(BF16)

    chips = (x, (x + 1) % 4, (x + 3) % 4, far_x)

    def chip_rows(i):
        return pl.ds(pl.multiple_of(chips[i] * 512, 512), 512)

    def first_term(j):
        for i in range(4):
            term[j, i] = dot(tr[j, chip_rows(i), :], gram[j])

    for copy in load_ranks:
        copy.wait()
    local_products(0)
    load_x.wait()
    x_second = gather_second(0, x_view, x_first)
    load_d.wait()
    d_first, d_second, d_relay = {}, {}, {}
    for p in (3, 2, 1, 0):

        @pl.when(x != p)
        def _():
            part = dm.at[p, k, z, y, :, pl.ds(0, 512 * (p + 1))]
            remote("diag", part, part, d_send.at[0], d_recv.at[p], far).wait_recv()

        d_first[p] = gather_first(2 + p, [d_view[p](h, z, y) for h in range(2)], d_view[p])
    local_products(1)
    panel_pass(0, 0)
    local_products(2)
    x_relay = gather_relay(0, x_view, x_second)
    for p in (3, 2, 1, 0):
        d_second[p] = gather_second(2 + p, d_view[p], d_first[p])
    panel_pass(0, 1)
    local_products(3)
    load_cr.wait()
    load_cl.wait()
    load_tr.wait()
    first_term(0)
    panel_pass(0, 2)
    first_term(1)
    first_term(2)
    panel_pass(0, 3)
    first_term(3)
    wait_all(x_relay)
    for p in (3, 2, 1, 0):
        d_relay[p] = gather_relay(2 + p, d_view[p], d_second[p])
    load_l.wait()
    l_second = gather_direct(1, l_view, l_first)
    panel_pass(1, 0)
    shares = {3: diag_share(3)}
    solve(3, k)
    shares[2] = diag_share(2)
    solve(2, k)
    panel_pass(1, 1)
    shares.update({p: diag_share(p) for p in (1, 0)})
    for p in (3, 2):
        shares[p].wait_recv()
        solve(p, 1 - k)
        solve_back(p)
        panel_pass(1, 5 - p)
    for p in (1, 0):
        shares[p].wait_recv()
        solve_both(p)
        solve_back(p)

    wait_all(l_second)
    for j in range(4):
        proj[j] = tdot(rl[...].reshape(2048, 256), tl[j]).astype(BF16)
        panel_far(0, j)
    for j in range(4):
        panel_sibling(0, j, (OWN_SIB, BACK_SIB, AHEAD_SIB, FAR_SIB))
        g = dot(yt[...], cr[j].reshape(2048, 256))
        keep = (lax.broadcasted_iota(jnp.int32, (256, 256), 0) < row_ranks[0]) & (
            lax.broadcasted_iota(jnp.int32, (256, 256), 1) < rank_c[j]
        )
        coupling = jnp.where(keep, g, 0.0).astype(BF16)
        cm = tdot(coupling, proj[j])
        keep = lax.broadcasted_iota(jnp.int32, (256, 256), 1) < rank_n[0, j]
        comb[j] = jnp.where(keep, cm, 0.0).astype(BF16)

    def update(i, j):
        second = dot(cl[j, i].reshape(512, 256), comb[j])
        out[0, j, chip_rows(i), :] = (term[j, i] - second).astype(BF16)

    for j in range(4):
        panel_far(1, j)
        panel_sibling(1, j, (OWN_SIB, BACK_SIB, AHEAD_SIB))
        for i in range(3):
            update(i, j)
    for j in range(4):
        panel_sibling(1, j, (FAR_SIB,))
        update(3, j)

    for p in range(4):

        @pl.when(x == p)
        def _():
            for n in range(3):
                part = dm.at[p, k, z, y, :, pl.ds(0, 512 * (p + 1))]
                remote("diag", part, part, d_send.at[n], d_recv.at[p], far).wait_send()

    for copy in pending:
        copy.wait_send()
    for t in range(2):
        for j in range(4):
            for kind in range(7):
                panel_copy(kind, t, j).wait_send()


def on_device(
    diag_inverse, row_left, row_right, col_left, col_right, row_ranks, col_ranks, tile_left, tile_right, new_ranks
):
    hbm = pl.BlockSpec(memory_space=pltpu.HBM)
    operands = (
        col_ranks, new_ranks, diag_inverse, row_left, row_right, col_left, col_right, tile_left, tile_right
    )
    dma = pltpu.SemaphoreType.DMA
    return pl.pallas_call(
        kernel,
        out_shape=pltpu.VMEM(tile_right.shape, tile_right.dtype),
        in_specs=[pl.BlockSpec(memory_space=pltpu.SMEM)] + [hbm] * 9,
        out_specs=pl.BlockSpec(memory_space=pltpu.VMEM),
        scratch_shapes=[
            pltpu.VMEM((4, 2048, 256), BF16),
            pltpu.VMEM((4, 2048, 256), BF16),
            pltpu.VMEM((4, 8, 256, 256), BF16),
            pltpu.VMEM((4, 4, 2, 256, 256), BF16),
            pltpu.VMEM((4, 4, 128, 256), BF16),
            pltpu.VMEM((4, 4, 128, 256), BF16),
            pltpu.VMEM((4, 2, 256, 256), BF16),
            pltpu.VMEM((256, 2048), BF16),
            pltpu.VMEM((4, 2, 4, 4, 16, 2048), BF16),
            pltpu.VMEM((4, 256, 256), BF16),
            pltpu.VMEM((4, 256, 256), BF16),
            pltpu.VMEM((4, 256, 256), BF16),
            pltpu.VMEM((4, 4, 512, 256), F32),
            pltpu.SMEM((4,), jnp.int32),
            pltpu.SMEM((1, 4), jnp.int32),
            dma((12,)),
            dma((7, 8)),
            dma((7, 8)),
            dma((3,)),
            dma((4,)),
            dma((4,)),
            dma((4,)),
            dma((6, 18)),
            dma((6, 18)),
        ],
        compiler_params=pltpu.CompilerParams(
            collective_id=0, has_side_effects=True, vmem_limit_bytes=52 * 1024 * 1024
        ),
        name="panel_step",
    )(row_ranks, *[pltpu.with_memory_space_constraint(a, pltpu.HBM) for a in operands])


def solution(mesh):
    in_specs = (
        P(("row", "col"), None),
        P("row", "col", None),
        P("row", "col", None),
        P("col", "row", None),
        P("col", "row", None),
        P("row"),
        P("col"),
        P("row", "col", None, None),
        P("row", "col", None, None),
        P("row", "col"),
    )
    out_specs = P("row", "col", None, None)
    return jax.shard_map(on_device, mesh=mesh, in_specs=in_specs, out_specs=out_specs, check_vma=False)
```
